512 devices in a mesh: frame: 64 (over y, z_lo, core), space: 8 (over x, z_hi).
Axes of the slice: x: 4, y: 8, z: 8 (z_hi: 2, z_lo: 4; z = z_hi * 4 + z_lo), core: 2. Of those that a mesh axis runs over, the one named last changes fastest.
Arguments:
- queries: bfloat16 [65536, 3072], P(('frame', 'space')), may hold values from -60 to 60
- keys: bfloat16 [65536, 3072], P(('frame', 'space')), may hold values from -6 to 6
- values: bfloat16 [65536, 3072], P(('frame', 'space')), may hold values from -6 to 6
- latent: bfloat16 [65536, 3072], P(('frame', 'space')), may hold values from -6 to 6
- step_gate: float32 [50, 3072], replicated, may hold values from 0.5 to 3
- levels: int32 [64], replicated, may hold values from 0 to 49
- context_start: int32 [64], replicated, may hold values from 0 to 7
- context_end: int32 [64], replicated, may hold values from 9 to 16
Outputs:
- queued: bfloat16 [65536, 3072], P(('frame', 'space'))
The draws below stay inside these ranges and needn't reach their ends.
All inputs are finite; a program needn't handle non-finite values.
Results may differ from the reference program's by a relative error of at most 0.0034.
Values may be sent and summed in bfloat16 or wider, within the bound.
A program may use at most 64 MiB of HBM per device.

```python
import math
import jax
import jax.numpy as jnp
from jax import lax

HEADS = 24
HEAD_DIM = 128
D = 3072
FRAMES_BLK = 16
LEVELS = 50
BLOCK_TOK = 1024
FRAME_TOK = 64
BLOCKS = 64
TOKENS = 65536


def draw_keys(key, part):
    key = jax.random.fold_in(key, 3)
    raw = jnp.clip(jax.random.normal(key, (TOKENS, D), jnp.float32), -6.0, 6.0)
    return raw.astype(jnp.bfloat16)


def draw_queries(key, part):
    key = jax.random.fold_in(key, 5)
    own = 2.0 * jnp.clip(jax.random.normal(key, (TOKENS, D), jnp.float32), -6.0, 6.0)
    return own.astype(jnp.bfloat16)


def draw_context_start(key, part):
    key = jax.random.fold_in(key, 11)
    spot_key, draw_key = jax.random.split(key)
    drawn = jax.random.randint(draw_key, (BLOCKS,), 0, FRAMES_BLK // 2, jnp.int32)
    spot = jax.random.randint(spot_key, (), 0, BLOCKS, jnp.int32)
    index = jnp.arange(BLOCKS, dtype=jnp.int32)
    drawn = jnp.where(index == spot, 0, drawn)
    return jnp.where(index == (spot + 1) % BLOCKS, FRAMES_BLK // 2 - 1, drawn).astype(jnp.int32)


def draw_context_end(key, part):
    key = jax.random.fold_in(key, 23)
    spot_key, draw_key = jax.random.split(key)
    drawn = jax.random.randint(draw_key, (BLOCKS,), FRAMES_BLK // 2 + 1, FRAMES_BLK + 1, jnp.int32)
    spot = jax.random.randint(spot_key, (), 0, BLOCKS, jnp.int32)
    index = jnp.arange(BLOCKS, dtype=jnp.int32)
    drawn = jnp.where(index == spot, FRAMES_BLK, drawn)
    return jnp.where(index == (spot + 1) % BLOCKS, FRAMES_BLK // 2 + 1, drawn).astype(jnp.int32)


def with_ends(values, own_key, smallest, largest):
    extent = values.shape
    spot = [jax.random.randint(jax.random.fold_in(own_key, axis), (), 0, extent[axis]) for axis in range(len(extent))]
    values = values.at[tuple(spot)].set(smallest)
    longest = extent.index(max(extent))
    spot[longest] = (spot[longest] + 1) % extent[longest]
    return values.at[tuple(spot)].set(largest)


def level_of(stream_key, shape, cuts, least, largest):
    def one(position, parts):
        heights = jax.random.uniform(jax.random.fold_in(jax.random.fold_in(stream_key, 6), position), (parts,), jnp.float32, least / len(cuts), largest / len(cuts))
        return jnp.repeat(jnp.exp(heights), shape[position] // parts).reshape((-1,) + (1,) * (len(shape) - position - 1))

    loudness = one(*cuts[0])
    for cut in cuts[1:]:
        loudness = loudness * one(*cut)
    return loudness


def gaussian(stream_key, dims, spread, bound, shards=(), held_as=jnp.bfloat16):
    array = spread * jax.random.normal(stream_key, dims, jnp.float32)
    if shards:
        array = array * level_of(stream_key, dims, shards, -0.22, 0.18)
    return jnp.clip(array, -bound, bound).astype(held_as)


def setup_inputs(seed: int = 0) -> dict:
    seeds = jax.random.split(jax.random.key(seed), 9)
    queries = draw_queries(jax.random.fold_in(seeds[8], 71), 0)
    keys = draw_keys(jax.random.fold_in(seeds[8], 71), 0)
    values = gaussian(seeds[2], (TOKENS, D), 1.0, 6.0, ((0, 512),))
    latent = gaussian(seeds[3], (TOKENS, D), 1.0, 6.0, ((0, 512),))
    step_gate = jnp.clip(jnp.exp(jax.random.uniform(seeds[4], (LEVELS, D), jnp.float32, math.log(0.5), math.log(3.0))), 0.5, 3.0)
    levels = with_ends(jax.random.randint(seeds[5], (BLOCKS,), 0, LEVELS), jax.random.fold_in(seeds[5], 1), 0, LEVELS - 1).astype(jnp.int32)
    context_start = draw_context_start(jax.random.fold_in(seeds[8], 71), 0)
    context_end = draw_context_end(jax.random.fold_in(seeds[8], 71), 0)
    return dict(queries=queries, keys=keys, values=values, latent=latent, step_gate=step_gate, levels=levels, context_start=context_start, context_end=context_end)


def reference(queries, keys, values, latent, step_gate, levels, context_start, context_end):
    scale = HEAD_DIM ** -0.5
    pad = ((BLOCK_TOK, BLOCK_TOK), (0, 0))
    keys_pad = jnp.pad(keys, pad)
    values_pad = jnp.pad(values, pad)
    column = jnp.arange(3 * BLOCK_TOK, dtype=jnp.int32)

    def one_block(block):
        start = (block * BLOCK_TOK).astype(jnp.int32)
        q_rows = lax.dynamic_slice_in_dim(queries, start, BLOCK_TOK, 0)
        k_rows = lax.dynamic_slice_in_dim(keys_pad, start, 3 * BLOCK_TOK, 0)
        v_rows = lax.dynamic_slice_in_dim(values_pad, start, 3 * BLOCK_TOK, 0)
        lat_rows = lax.dynamic_slice_in_dim(latent, start, BLOCK_TOK, 0)
        first = context_start[block] * FRAME_TOK
        last = context_end[block] * FRAME_TOK
        before = (column < BLOCK_TOK) & (column >= first) & (block > 0)
        inside = (column >= BLOCK_TOK) & (column < 2 * BLOCK_TOK)
        after = (column >= 2 * BLOCK_TOK) & (column - 2 * BLOCK_TOK < last) & (block < BLOCKS - 1)
        visible = before | inside | after
        pieces = []
        for head in range(HEADS):
            lo = head * HEAD_DIM
            hi = lo + HEAD_DIM
            scores = jnp.dot(q_rows[:, lo:hi], k_rows[:, lo:hi].T, preferred_element_type=jnp.float32) * scale
            scores = jnp.where(visible[None, :], scores, -1e30)
            top = jnp.max(scores, axis=1, keepdims=True)
            expo = jnp.exp(scores - top)
            weights = (expo / jnp.sum(expo, axis=1, keepdims=True)).astype(jnp.bfloat16)
            pieces.append(jnp.dot(weights, v_rows[:, lo:hi], preferred_element_type=jnp.float32).astype(jnp.bfloat16))
        attended = jnp.concatenate(pieces, axis=1)
        gate = step_gate[levels[block]]
        return (lat_rows.astype(jnp.float32) + gate[None, :] * attended.astype(jnp.float32)).astype(jnp.bfloat16)

    updated = lax.map(one_block, jnp.arange(BLOCKS, dtype=jnp.int32))
    moved = jnp.concatenate([jnp.zeros((1, BLOCK_TOK, D), jnp.bfloat16), updated[:-1]], axis=0)
    return moved.reshape(TOKENS, D)
```

```python
import functools

import jax
import jax.numpy as jnp
from jax import lax
from jax.experimental import pallas as pl
from jax.experimental.pallas import tpu as pltpu
from jax.sharding import PartitionSpec as P

HEAD_DIM = 128
FRAME_TOK = 64
SLICE = 128
BLOCK = 1024
LOCAL_HEADS = 3
GROUP = LOCAL_HEADS * HEAD_DIM
Q_ROWS = 256
CHUNKS = BLOCK // Q_ROWS
LOG2E = 1.4426950408889634
SCALE2 = HEAD_DIM ** (-0.5) * LOG2E
HIDDEN = -1e30
MESH = pl.DeviceIdType.MESH
DISTANCES = (4, 3, 5, 2, 6, 1, 7, 0)


def wrap(a, n):
    return lax.rem(a + n, n)


def position():
    frame, space = lax.axis_index("frame"), lax.axis_index("space")
    return space // 2, frame // 8, lax.rem(frame // 2, 4) + 4 * lax.rem(space, 2), lax.rem(frame, 2)


def device(x, y, z, core):
    return (y * 8 + lax.rem(z, 4) * 2 + core, x * 2 + z // 4)


def following(pair, y, core):
    return (
        wrap(pair + core, 4),
        wrap(y + core * (pair // 3), 8),
        1 - core,
    )


def preceding(pair, y, core):
    back = 1 - core
    return (
        wrap(pair - back, 4),
        wrap(y - back * ((3 - pair) // 3), 8),
        1 - core,
    )


def worker(pair, y, core, group):
    return device(lax.rem(pair + group, 4), y, group, core)


def kernel(
    start_ref, end_ref, q_hbm, k_hbm, v_hbm, latent_hbm,
    att_hbm, lat_out_hbm,
    q_buf, k_buf, v_buf, o_buf, p_buf,
    in_send, in_recv, near_send, near_recv, o_send, o_recv, lat_send, lat_recv,
):
    x, y, z, core = position()
    z_lo, z_hi = lax.rem(z, 4), z // 4
    here = x * 2 + z_hi
    pair = wrap(x - lax.rem(z, 4), 4)
    block = y * 8 + pair * 2 + core
    after, before = following(pair, y, core), preceding(pair, y, core)
    next_worker, prev_worker = worker(*after, z), worker(*before, z)
    home_after, home_before = following(z_lo, y, core), preceding(z_lo, y, core)
    keeps = x == wrap(2 * z_lo, 4)

    def home(spot, slice_index):
        p, yy, cc = spot
        return device(slice_index // 2, yy, p + 4 * lax.rem(slice_index, 2), cc)

    barrier = pltpu.get_barrier_semaphore()

    def greet(target):
        pl.semaphore_signal(barrier, inc=1, device_id=target, device_id_type=MESH)

    for t in range(8):
        source = home((pair, y, core), t)
        pl.when(jnp.logical_not(keeps & (here == t)))(functools.partial(greet, source))
        greet(worker(*home_before, t))
    greet(prev_worker)
    greet(next_worker)
    greet(home(home_before, here))
    pl.semaphore_wait(barrier, jnp.where(keeps, 18, 19))

    arrays = ((k_hbm, k_buf, BLOCK), (v_hbm, v_buf, BLOCK), (q_hbm, q_buf, 0))

    def incoming(which, h, i):
        hbm, buf, row0 = arrays[which]
        group = lax.rem(z + DISTANCES[i], 8)
        return (
            hbm.at[:, pl.ds(pl.multiple_of(group * GROUP + h * HEAD_DIM, HEAD_DIM), HEAD_DIM)],
            buf.at[h, pl.ds(pl.multiple_of(row0 + here * SLICE, SLICE), SLICE)],
            worker(z_lo, y, core, group),
        )

    def in_copy(which, h, i):
        src, dst, target = incoming(which, h, i)
        return pltpu.make_async_remote_copy(
            src_ref=src, dst_ref=dst, send_sem=in_send.at[which, h, i], recv_sem=in_recv.at[which, h],
            device_id=target, device_id_type=MESH,
        )

    def own_copy(which, h, i):
        src, dst, _ = incoming(which, h, i)
        return pltpu.make_async_copy(src, dst, in_recv.at[which, h])

    for h in range(LOCAL_HEADS):
        for which in range(3):
            for i, distance in enumerate(DISTANCES):
                if distance == 0:
                    pl.when(keeps)(lambda: own_copy(which, h, i).start())
                    pl.when(jnp.logical_not(keeps))(lambda: in_copy(which, h, i).start())
                else:
                    in_copy(which, h, i).start()

    lat_copy = pltpu.make_async_remote_copy(
        src_ref=latent_hbm, dst_ref=lat_out_hbm, send_sem=lat_send, recv_sem=lat_recv,
        device_id=home(home_after, here), device_id_type=MESH,
    )
    lat_copy.start()

    def wait_in(which, h):
        _, buf, row0 = arrays[which]
        whole = buf.at[h, pl.ds(row0, BLOCK)]
        pltpu.make_async_copy(whole, whole, in_recv.at[which, h]).wait()

    def near_copy(which, h, side):
        _, buf, _ = arrays[which]
        return pltpu.make_async_remote_copy(
            src_ref=buf.at[h, pl.ds(BLOCK, BLOCK)],
            dst_ref=buf.at[h, pl.ds(0 if side else 2 * BLOCK, BLOCK)],
            send_sem=near_send.at[which, h, side], recv_sem=near_recv.at[which, h, side],
            device_id=next_worker if side else prev_worker, device_id_type=MESH,
        )

    def pass_on(which, h):
        wait_in(which, h)
        for side in range(2):
            near_copy(which, h, side).start()

    def o_copy(h, t):
        return pltpu.make_async_remote_copy(
            src_ref=o_buf.at[h, pl.ds(pl.multiple_of(t * SLICE, SLICE), SLICE)],
            dst_ref=att_hbm.at[:, pl.ds(pl.multiple_of(z * GROUP + h * HEAD_DIM, HEAD_DIM), HEAD_DIM)],
            send_sem=o_send.at[h, t], recv_sem=o_recv.at[h],
            device_id=home(after, t), device_id_type=MESH,
        )

    pass_on(0, 0)
    pass_on(1, 0)

    column = lax.broadcasted_iota(jnp.int32, (1, BLOCK), 1)
    first = start_ref[block] * FRAME_TOK
    last = end_ref[block] * FRAME_TOK
    hide_before = jnp.where((column >= first) & (block > 0), 0.0, HIDDEN)
    hide_after = jnp.where((column < last) & (block < 63), 0.0, HIDDEN)

    def step(n, carry):
        h, i = n // CHUNKS, lax.rem(n, CHUNKS)

        @pl.when(i == 0)
        def _():
            wait_in(2, h)
            for which in range(2):
                for side in range(2):
                    near_copy(which, h, side).wait_recv()

        for which in range(2):
            pl.when((i == 2 + which) & (h < LOCAL_HEADS - 1))(lambda: pass_on(which, h + 1))

        chunk = lax.rem(i + x + z, CHUNKS)
        rows = pl.ds(pl.multiple_of(chunk * Q_ROWS, Q_ROWS), Q_ROWS)
        q = q_buf[h, rows, :]
        parts = []
        for part, hide in ((0, hide_before), (1, None), (2, hide_after)):
            s = lax.dot_general(
                q, k_buf[h, pl.ds(part * BLOCK, BLOCK), :], (((1,), (1,)), ((), ())),
                preferred_element_type=jnp.float32,
            ) * SCALE2
            parts.append(s if hide is None else s + hide)
        top = functools.reduce(jnp.maximum, [jnp.max(s, axis=1, keepdims=True) for s in parts])
        parts = [jnp.exp2(s - top) for s in parts]
        total = sum(jnp.sum(e, axis=1, keepdims=True) for e in parts)
        inverse = 1.0 / total
        out = None
        for part, e in enumerate(parts):
            o = jnp.dot(
                (e * inverse).astype(jnp.bfloat16), v_buf[h, pl.ds(part * BLOCK, BLOCK), :],
                preferred_element_type=jnp.float32,
            )
            out = o if out is None else out + o
        o_buf[h, rows, :] = out.astype(jnp.bfloat16)
        for t in range(Q_ROWS // SLICE):
            o_copy(h, chunk * (Q_ROWS // SLICE) + t).start()
        return carry

    lax.fori_loop(0, LOCAL_HEADS * CHUNKS, step, 0)

    for h in range(LOCAL_HEADS):
        pltpu.make_async_copy(o_buf.at[h], o_buf.at[h], o_recv.at[h]).wait()
    lat_copy.wait()
    for h in range(LOCAL_HEADS):
        for t in range(8):
            o_copy(h, t).wait_send()
        for which in range(3):
            for i, distance in enumerate(DISTANCES):
                if distance == 0:
                    pl.when(jnp.logical_not(keeps))(lambda: in_copy(which, h, i).wait_send())
                else:
                    in_copy(which, h, i).wait_send()
            if which < 2:
                for side in range(2):
                    near_copy(which, h, side).wait_send()


def on_device(queries, keys, values, latent, step_gate, levels, context_start, context_end):
    any_spec = pl.BlockSpec(memory_space=pl.ANY)
    smem = pl.BlockSpec(memory_space=pltpu.SMEM)
    dma = pltpu.SemaphoreType.DMA
    rows = jax.ShapeDtypeStruct(latent.shape, jnp.bfloat16)
    attended, moved = pl.pallas_call(
        kernel,
        out_shape=(rows, rows),
        in_specs=[smem, smem] + [any_spec] * 4,
        out_specs=(any_spec, any_spec),
        scratch_shapes=[
            pltpu.VMEM((LOCAL_HEADS, BLOCK, HEAD_DIM), jnp.bfloat16),
            pltpu.VMEM((LOCAL_HEADS, 3 * BLOCK, HEAD_DIM), jnp.bfloat16),
            pltpu.VMEM((LOCAL_HEADS, 3 * BLOCK, HEAD_DIM), jnp.bfloat16),
            pltpu.VMEM((LOCAL_HEADS, BLOCK, HEAD_DIM), jnp.bfloat16),
            pltpu.VMEM((16, 128), jnp.bfloat16),
            dma((3, LOCAL_HEADS, 8)), dma((3, LOCAL_HEADS)),
            dma((2, LOCAL_HEADS, 2)), dma((2, LOCAL_HEADS, 2)),
            dma((LOCAL_HEADS, 8)), dma((LOCAL_HEADS,)),
            dma, dma,
        ],
        compiler_params=pltpu.CompilerParams(
            collective_id=0, has_side_effects=True, vmem_limit_bytes=48 << 20
        ),
        cost_estimate=pl.CostEstimate(flops=4 * BLOCK * 3 * BLOCK * GROUP, bytes_accessed=8 << 20, transcendentals=0),
        name="attend",
    )(context_start, context_end, queries, keys, values, latent)
    frame = lax.axis_index("frame")
    gate = step_gate[levels[jnp.maximum(frame - 1, 0)]]
    updated = moved.astype(jnp.float32) + gate[None, :] * attended.astype(jnp.float32)
    return jnp.where(frame > 0, updated, 0.0).astype(jnp.bfloat16)


def solution(mesh):
    tokens = P(("frame", "space"), None)
    return jax.shard_map(
        on_device,
        mesh=mesh,
        in_specs=(tokens,) * 4 + (P(),) * 4,
        out_specs=tokens,
        check_vma=False,
    )
```

```python
import functools

import jax
import jax.numpy as jnp
from jax import lax
from jax.experimental import pallas as pl
from jax.experimental.pallas import tpu as pltpu
from jax.sharding import PartitionSpec as P

HEAD_DIM = 128
FRAME_TOK = 64
SLICE = 128
BLOCK = 1024
LOCAL_HEADS = 3
GROUP = LOCAL_HEADS * HEAD_DIM
Q_ROWS = 256
CHUNKS = BLOCK // Q_ROWS
LOG2E = 1.4426950408889634
SCALE2 = HEAD_DIM ** (-0.5) * LOG2E
HIDDEN = -1e30
KEYS, VALUES, QUERIES = 0, 1, 2
MESH = pl.DeviceIdType.MESH
DISTANCES = (4, 3, 5, 2, 6, 1, 7, 0)


def wrap(a, n):
    return lax.rem(a + n, n)


def position():
    frame, space = lax.axis_index("frame"), lax.axis_index("space")
    return space // 2, frame // 8, lax.rem(frame // 2, 4) + 4 * lax.rem(space, 2), lax.rem(frame, 2)


def device(x, y, z, core):
    return (y * 8 + lax.rem(z, 4) * 2 + core, x * 2 + z // 4)


def following(pair, y, core):
    return (
        wrap(pair + core, 4),
        wrap(y + core * (pair // 3), 8),
        1 - core,
    )


def preceding(pair, y, core):
    back = 1 - core
    return (
        wrap(pair - back, 4),
        wrap(y - back * ((3 - pair) // 3), 8),
        1 - core,
    )


def worker(pair, y, core, group):
    return device(lax.rem(pair + group, 4), y, group, core)


def kernel(
    start_hbm, end_hbm, levels_hbm, gate_hbm, q_hbm, k_hbm, v_hbm, latent_hbm,
    att_hbm, lat_out_hbm, gate_ref,
    q_buf, k_buf, v_buf, o_buf, gate_buf, start_ref, end_ref, levels_ref,
    in_send, in_recv, near_send, near_recv, o_send, o_recv, lat_send, lat_recv, table_sem,
):
    x, y, z, core = position()
    z_lo, z_hi = lax.rem(z, 4), z // 4
    here = x * 2 + z_hi
    pair = wrap(x - lax.rem(z, 4), 4)
    block = y * 8 + pair * 2 + core
    after, before = following(pair, y, core), preceding(pair, y, core)
    next_worker, prev_worker = worker(*after, z), worker(*before, z)
    home_after, home_before = following(z_lo, y, core), preceding(z_lo, y, core)
    keeps = x == wrap(2 * z_lo, 4)

    def home(spot, slice_index):
        p, yy, cc = spot
        return device(slice_index // 2, yy, p + 4 * lax.rem(slice_index, 2), cc)

    tables = [
        pltpu.make_async_copy(src, dst, table_sem.at[i])
        for i, (src, dst) in enumerate(
            ((start_hbm, start_ref), (end_hbm, end_ref), (levels_hbm, levels_ref), (gate_hbm, gate_buf))
        )
    ]
    barrier = pltpu.get_barrier_semaphore()

    def greet(target):
        pl.semaphore_signal(barrier, inc=1, device_id=target, device_id_type=MESH)

    for t in range(8):
        source = home((pair, y, core), t)
        pl.when(jnp.logical_not(keeps & (here == t)))(functools.partial(greet, source))
        greet(worker(*home_before, t))
    greet(prev_worker)
    greet(next_worker)
    greet(home(home_before, here))
    pl.semaphore_wait(barrier, jnp.where(keeps, 18, 19))

    arrays = ((k_hbm, k_buf, BLOCK), (v_hbm, v_buf, BLOCK), (q_hbm, q_buf, 0))

    def incoming(which, h, i):
        hbm, buf, row0 = arrays[which]
        group = lax.rem(z + DISTANCES[i], 8)
        return (
            hbm.at[:, pl.ds(pl.multiple_of(group * GROUP + h * HEAD_DIM, HEAD_DIM), HEAD_DIM)],
            buf.at[h, pl.ds(pl.multiple_of(row0 + here * SLICE, SLICE), SLICE)],
            worker(z_lo, y, core, group),
        )

    def in_copy(which, h, i):
        src, dst, target = incoming(which, h, i)
        return pltpu.make_async_remote_copy(
            src_ref=src, dst_ref=dst, send_sem=in_send.at[which, h, i], recv_sem=in_recv.at[which, h],
            device_id=target, device_id_type=MESH,
        )

    def own_copy(which, h, i):
        src, dst, _ = incoming(which, h, i)
        return pltpu.make_async_copy(src, dst, in_recv.at[which, h])

    def send_in(which, h):
        for i, distance in enumerate(DISTANCES):
            if distance == 0:
                pl.when(keeps)(lambda: own_copy(which, h, i).start())
                pl.when(jnp.logical_not(keeps))(lambda: in_copy(which, h, i).start())
            else:
                in_copy(which, h, i).start()

    lat_copy = pltpu.make_async_remote_copy(
        src_ref=latent_hbm, dst_ref=lat_out_hbm, send_sem=lat_send, recv_sem=lat_recv,
        device_id=home(home_after, here), device_id_type=MESH,
    )
    def wait_in(which, h):
        _, buf, row0 = arrays[which]
        whole = buf.at[h, pl.ds(row0, BLOCK)]
        pltpu.make_async_copy(whole, whole, in_recv.at[which, h]).wait()

    def near_copy(which, h, side):
        _, buf, _ = arrays[which]
        return pltpu.make_async_remote_copy(
            src_ref=buf.at[h, pl.ds(BLOCK, BLOCK)],
            dst_ref=buf.at[h, pl.ds(0 if side else 2 * BLOCK, BLOCK)],
            send_sem=near_send.at[which, h, side], recv_sem=near_recv.at[which, h, side],
            device_id=next_worker if side else prev_worker, device_id_type=MESH,
        )

    def pass_on(which, h):
        wait_in(which, h)
        for side in range(2):
            near_copy(which, h, side).start()

    def o_copy(h, t):
        return pltpu.make_async_remote_copy(
            src_ref=o_buf.at[h, pl.ds(pl.multiple_of(t * SLICE, SLICE), SLICE)],
            dst_ref=att_hbm.at[:, pl.ds(pl.multiple_of(z * GROUP + h * HEAD_DIM, HEAD_DIM), HEAD_DIM)],
            send_sem=o_send.at[h, t], recv_sem=o_recv.at[h],
            device_id=home(after, t), device_id_type=MESH,
        )

    send_in(KEYS, 0)
    send_in(VALUES, 0)
    send_in(QUERIES, 0)
    send_in(KEYS, 1)
    for copy in tables:
        copy.start()
    pass_on(KEYS, 0)
    send_in(VALUES, 1)
    pass_on(VALUES, 0)
    send_in(QUERIES, 1)
    for copy in tables:
        copy.wait()
    gate_ref[...] = gate_buf[pl.ds(levels_ref[wrap(lax.axis_index("frame") - 1, 64)], 1), :]

    column = lax.broadcasted_iota(jnp.int32, (1, BLOCK), 1)
    first = start_ref[block] * FRAME_TOK
    last = end_ref[block] * FRAME_TOK
    hide_before = jnp.where((column >= first) & (block > 0), 0.0, HIDDEN)
    hide_after = jnp.where((column < last) & (block < 63), 0.0, HIDDEN)

    def step(n, carry):
        h, i = n // CHUNKS, lax.rem(n, CHUNKS)

        @pl.when(i == 0)
        def _():
            wait_in(QUERIES, h)
            for which in range(2):
                for side in range(2):
                    near_copy(which, h, side).wait_recv()

        @pl.when((i == 2) & (h < LOCAL_HEADS - 1))
        def _():
            pass_on(KEYS, h + 1)
            pl.when(h == 0)(lambda: send_in(KEYS, 2))
            pl.when(h == 1)(lambda: send_in(QUERIES, 2))

        @pl.when((i == 3) & (h < LOCAL_HEADS - 1))
        def _():
            pass_on(VALUES, h + 1)
            pl.when(h == 0)(lambda: send_in(VALUES, 2))
            pl.when(h == 1)(lambda: lat_copy.start())

        chunk = lax.rem(i + x + z, CHUNKS)
        rows = pl.ds(pl.multiple_of(chunk * Q_ROWS, Q_ROWS), Q_ROWS)
        q = q_buf[h, rows, :]
        parts = []
        for part, hide in ((0, hide_before), (1, None), (2, hide_after)):
            s = lax.dot_general(
                q, k_buf[h, pl.ds(part * BLOCK, BLOCK), :], (((1,), (1,)), ((), ())),
                preferred_element_type=jnp.float32,
            ) * SCALE2
            parts.append(s if hide is None else s + hide)
        top = functools.reduce(jnp.maximum, [jnp.max(s, axis=1, keepdims=True) for s in parts])
        parts = [jnp.exp2(s - top) for s in parts]
        total = sum(jnp.sum(e, axis=1, keepdims=True) for e in parts)
        inverse = 1.0 / total
        out = None
        for part, e in enumerate(parts):
            o = jnp.dot(
                (e * inverse).astype(jnp.bfloat16), v_buf[h, pl.ds(part * BLOCK, BLOCK), :],
                preferred_element_type=jnp.float32,
            )
            out = o if out is None else out + o
        o_buf[h, rows, :] = out.astype(jnp.bfloat16)
        for t in range(Q_ROWS // SLICE):
            o_copy(h, chunk * (Q_ROWS // SLICE) + t).start()
        return carry

    lax.fori_loop(0, LOCAL_HEADS * CHUNKS, step, 0)

    for h in range(LOCAL_HEADS):
        pltpu.make_async_copy(o_buf.at[h], o_buf.at[h], o_recv.at[h]).wait()
    lat_copy.wait()
    for h in range(LOCAL_HEADS):
        for t in range(8):
            o_copy(h, t).wait_send()
        for which in range(3):
            for i, distance in enumerate(DISTANCES):
                if distance == 0:
                    pl.when(jnp.logical_not(keeps))(lambda: in_copy(which, h, i).wait_send())
                else:
                    in_copy(which, h, i).wait_send()
            if which < 2:
                for side in range(2):
                    near_copy(which, h, side).wait_send()


def run_kernel(
    context_start, context_end, queries, keys, values, latent, step_gate, levels, name="attend", cid=0
):
    any_spec = pl.BlockSpec(memory_space=pl.ANY)
    dma = pltpu.SemaphoreType.DMA
    rows = jax.ShapeDtypeStruct(latent.shape, jnp.bfloat16)
    return pl.pallas_call(
        kernel,
        out_shape=(rows, rows, jax.ShapeDtypeStruct((1, step_gate.shape[1]), jnp.float32)),
        in_specs=[any_spec] * 8,
        out_specs=(any_spec, any_spec, pl.BlockSpec(memory_space=pltpu.VMEM)),
        scratch_shapes=[
            pltpu.VMEM((LOCAL_HEADS, BLOCK, HEAD_DIM), jnp.bfloat16),
            pltpu.VMEM((LOCAL_HEADS, 3 * BLOCK, HEAD_DIM), jnp.bfloat16),
            pltpu.VMEM((LOCAL_HEADS, 3 * BLOCK, HEAD_DIM), jnp.bfloat16),
            pltpu.VMEM((LOCAL_HEADS, BLOCK, HEAD_DIM), jnp.bfloat16),
            pltpu.VMEM(step_gate.shape, jnp.float32),
            pltpu.SMEM(context_start.shape, jnp.int32),
            pltpu.SMEM(context_end.shape, jnp.int32),
            pltpu.SMEM(levels.shape, jnp.int32),
            dma((3, LOCAL_HEADS, 8)), dma((3, LOCAL_HEADS)),
            dma((2, LOCAL_HEADS, 2)), dma((2, LOCAL_HEADS, 2)),
            dma((LOCAL_HEADS, 8)), dma((LOCAL_HEADS,)),
            dma, dma, dma((4,)),
        ],
        compiler_params=pltpu.CompilerParams(
            collective_id=cid, has_side_effects=True, vmem_limit_bytes=61000 << 10
        ),
        cost_estimate=pl.CostEstimate(
            flops=4 * BLOCK * 3 * BLOCK * GROUP, bytes_accessed=8 << 20, transcendentals=0
        ),
        name=name,
    )(context_start, context_end, levels, step_gate, queries, keys, values, latent)


def on_device(queries, keys, values, latent, step_gate, levels, context_start, context_end):
    attended, moved, gate = run_kernel(
        context_start, context_end, queries, keys, values, latent, step_gate, levels
    )
    updated = moved.astype(jnp.float32) + gate * attended.astype(jnp.float32)
    return jnp.where(lax.axis_index("frame") > 0, updated, 0.0).astype(jnp.bfloat16)


def solution(mesh):
    tokens = P(("frame", "space"), None)
    return jax.shard_map(
        on_device,
        mesh=mesh,
        in_specs=(tokens,) * 4 + (P(),) * 4,
        out_specs=tokens,
        check_vma=False,
    )
```

```python
import functools

import jax
import jax.numpy as jnp
from jax import lax
from jax.experimental import pallas as pl
from jax.experimental.pallas import tpu as pltpu
from jax.sharding import PartitionSpec as P

HEAD_DIM = 128
FRAME_TOK = 64
SLICE = 128
BLOCK = 1024
LOCAL_HEADS = 3
GROUP = LOCAL_HEADS * HEAD_DIM
Q_ROWS = 256
CHUNKS = BLOCK // Q_ROWS
LOG2E = 1.4426950408889634
SCALE2 = HEAD_DIM ** (-0.5) * LOG2E
HIDDEN = -1e30
KEYS, VALUES, QUERIES = 0, 1, 2
MESH = pl.DeviceIdType.MESH
PEERS = 8
LAT_PARTS = 3
NEAR_PARTS = 8


def wrap(a, n):
    return lax.rem(a + n, n)


def position():
    frame, space = lax.axis_index("frame"), lax.axis_index("space")
    return space // 2, frame // 8, lax.rem(frame // 2, 4) + 4 * lax.rem(space, 2), lax.rem(frame, 2)


def device(x, y, z, core):
    return (y * 8 + lax.rem(z, 4) * 2 + core, x * 2 + z // 4)


def following(pair, y, core):
    return (
        wrap(pair + core, 4),
        wrap(y + core * (pair // 3), 8),
        1 - core,
    )


def preceding(pair, y, core):
    back = 1 - core
    return (
        wrap(pair - back, 4),
        wrap(y - back * ((3 - pair) // 3), 8),
        1 - core,
    )


def offset(group):
    return 2 * lax.rem(group, 2)


def worker(pair, y, core, group):
    return device(lax.rem(pair + offset(group), 4), y, group, core)


def kernel(
    start_hbm, end_hbm, levels_hbm, gate_hbm, q_hbm, k_hbm, v_hbm, latent_hbm,
    att_hbm, lat_out_hbm, gate_ref,
    q_buf, k_buf, v_buf, o_buf, gate_buf, start_ref, end_ref, levels_ref,
    in_send, in_recv, near_send, near_recv, o_send, o_recv, lat_send, lat_recv, table_sem,
):
    x, y, z, core = position()
    z_lo, z_hi = lax.rem(z, 4), z // 4
    here = x * 2 + z_hi
    pair = wrap(x - offset(z), 4)
    block = y * 8 + pair * 2 + core
    after, before = following(pair, y, core), preceding(pair, y, core)
    next_worker, prev_worker = worker(*after, z), worker(*before, z)
    home_after, home_before = following(z_lo, y, core), preceding(z_lo, y, core)
    keeps = x == lax.rem(z_lo + offset(z), 4)

    def home(spot, slice_index):
        p, yy, cc = spot
        return device(slice_index // 2, yy, p + 4 * lax.rem(slice_index, 2), cc)

    tables = [
        pltpu.make_async_copy(src, dst, table_sem.at[i])
        for i, (src, dst) in enumerate(
            ((start_hbm, start_ref), (end_hbm, end_ref), (levels_hbm, levels_ref), (gate_hbm, gate_buf))
        )
    ]
    barrier = pltpu.get_barrier_semaphore()

    def greet(target):
        pl.semaphore_signal(barrier, inc=1, device_id=target, device_id_type=MESH)

    for t in range(8):
        source = home((pair, y, core), t)
        pl.when(jnp.logical_not(keeps & (here == t)))(functools.partial(greet, source))
        greet(worker(*home_before, t))
    greet(prev_worker)
    greet(next_worker)
    greet(home(home_before, here))
    pl.semaphore_wait(barrier, jnp.where(keeps, 18, 19))

    arrays = ((k_hbm, k_buf, BLOCK), (v_hbm, v_buf, BLOCK), (q_hbm, q_buf, 0))

    def distance(i):
        turn = lax.rem(i // 2 + x, 4)
        along = 3 - turn if i % 2 else 4 + turn
        return lax.rem(jnp.where(core == 0, along, 8 - along), 8)

    def served(i, act_here, act_there):
        if i % 2:
            mine = keeps & (distance(i) == 0)
            pl.when(mine)(act_here)
            pl.when(jnp.logical_not(mine))(act_there)
        else:
            act_there()

    def incoming(which, h, i):
        hbm, buf, row0 = arrays[which]
        group = lax.rem(z + distance(i), 8)
        return (
            hbm.at[:, pl.ds(pl.multiple_of(group * GROUP + h * HEAD_DIM, HEAD_DIM), HEAD_DIM)],
            buf.at[h, pl.ds(pl.multiple_of(row0 + here * SLICE, SLICE), SLICE)],
            worker(z_lo, y, core, group),
        )

    def in_copy(which, h, i):
        src, dst, target = incoming(which, h, i)
        return pltpu.make_async_remote_copy(
            src_ref=src, dst_ref=dst, send_sem=in_send.at[which, h, i], recv_sem=in_recv.at[which, h],
            device_id=target, device_id_type=MESH,
        )

    def own_copy(which, h, i):
        src, dst, _ = incoming(which, h, i)
        return pltpu.make_async_copy(src, dst, in_recv.at[which, h])

    def send_in(which, h):
        for i in range(PEERS):
            served(i, lambda: own_copy(which, h, i).start(), lambda: in_copy(which, h, i).start())

    def lat_copy(part):
        width = latent_hbm.shape[1] // LAT_PARTS
        columns = pl.ds(pl.multiple_of(part * width, HEAD_DIM), width)
        return pltpu.make_async_remote_copy(
            src_ref=latent_hbm.at[:, columns], dst_ref=lat_out_hbm.at[:, columns],
            send_sem=lat_send.at[part], recv_sem=lat_recv.at[part],
            device_id=home(home_after, here), device_id_type=MESH,
        )

    def wait_in(which, h):
        _, buf, row0 = arrays[which]
        whole = buf.at[h, pl.ds(row0, BLOCK)]
        pltpu.make_async_copy(whole, whole, in_recv.at[which, h]).wait()

    def near_copy(which, h, side, row=0, rows=BLOCK):
        _, buf, _ = arrays[which]
        to = 0 if side else 2 * BLOCK
        return pltpu.make_async_remote_copy(
            src_ref=buf.at[h, pl.ds(BLOCK + row, rows)],
            dst_ref=buf.at[h, pl.ds(to + row, rows)],
            send_sem=near_send.at[which, h, side], recv_sem=near_recv.at[which, h, side],
            device_id=next_worker if side else prev_worker, device_id_type=MESH,
        )

    def pass_on(which, h):
        wait_in(which, h)
        for piece in range(NEAR_PARTS):
            for side in range(2):
                near_copy(which, h, side, piece * (BLOCK // NEAR_PARTS), BLOCK // NEAR_PARTS).start()

    def o_copy(h, t):
        return pltpu.make_async_remote_copy(
            src_ref=o_buf.at[h, pl.ds(pl.multiple_of(t * SLICE, SLICE), SLICE)],
            dst_ref=att_hbm.at[:, pl.ds(pl.multiple_of(z * GROUP + h * HEAD_DIM, HEAD_DIM), HEAD_DIM)],
            send_sem=o_send.at[h, t], recv_sem=o_recv.at[h],
            device_id=home(after, t), device_id_type=MESH,
        )

    for h in range(LOCAL_HEADS):
        for which in (KEYS, VALUES, QUERIES):
            send_in(which, h)
    for copy in tables:
        copy.start()
    pass_on(KEYS, 0)
    pass_on(VALUES, 0)
    lat_copy(0).start()
    for copy in tables:
        copy.wait()
    level = levels_ref[wrap(lax.axis_index("frame") - 1, 64)]
    gate_ref[...] = jnp.broadcast_to(gate_buf[pl.ds(level, 1), :], gate_ref.shape)

    column = lax.broadcasted_iota(jnp.int32, (1, BLOCK), 1)
    first = start_ref[block] * FRAME_TOK
    last = end_ref[block] * FRAME_TOK
    hide_before = jnp.where((column >= first) & (block > 0), 0.0, HIDDEN)
    hide_after = jnp.where((column < last) & (block < 63), 0.0, HIDDEN)

    def step(n, carry):
        h, i = n // CHUNKS, lax.rem(n, CHUNKS)

        @pl.when(i == 0)
        def _():
            wait_in(QUERIES, h)
            for which in range(2):
                for side in range(2):
                    near_copy(which, h, side).wait_recv()

        @pl.when((i == 2) & (h < LOCAL_HEADS - 1))
        def _():
            pass_on(KEYS, h + 1)

        @pl.when((i == 3) & (h < LOCAL_HEADS - 1))
        def _():
            pass_on(VALUES, h + 1)
            lat_copy(h + 1).start()

        chunk = lax.rem(i + x + z, CHUNKS)
        rows = pl.ds(pl.multiple_of(chunk * Q_ROWS, Q_ROWS), Q_ROWS)
        q = q_buf[h, rows, :]
        parts = []
        for part, hide in ((0, hide_before), (1, None), (2, hide_after)):
            s = lax.dot_general(
                q, k_buf[h, pl.ds(part * BLOCK, BLOCK), :], (((1,), (1,)), ((), ())),
                preferred_element_type=jnp.float32,
            ) * SCALE2
            parts.append(s if hide is None else s + hide)
        top = functools.reduce(jnp.maximum, [jnp.max(s, axis=1, keepdims=True) for s in parts])
        parts = [jnp.exp2(s - top) for s in parts]
        total = sum(jnp.sum(e, axis=1, keepdims=True) for e in parts)
        inverse = 1.0 / total
        out = None
        for part, e in enumerate(parts):
            o = jnp.dot(
                (e * inverse).astype(jnp.bfloat16), v_buf[h, pl.ds(part * BLOCK, BLOCK), :],
                preferred_element_type=jnp.float32,
            )
            out = o if out is None else out + o
        o_buf[h, rows, :] = out.astype(jnp.bfloat16)
        for t in range(Q_ROWS // SLICE):
            o_copy(h, chunk * (Q_ROWS // SLICE) + t).start()
        return carry

    lax.fori_loop(0, LOCAL_HEADS * CHUNKS, step, 0)

    for h in range(LOCAL_HEADS):
        pltpu.make_async_copy(o_buf.at[h], o_buf.at[h], o_recv.at[h]).wait()
    for part in range(LAT_PARTS):
        lat_copy(part).wait()
    for h in range(LOCAL_HEADS):
        for t in range(8):
            o_copy(h, t).wait_send()
        for which in range(3):
            for i in range(PEERS):
                served(i, lambda: None, lambda: in_copy(which, h, i).wait_send())
            if which < 2:
                for side in range(2):
                    near_copy(which, h, side).wait_send()


def run_kernel(
    context_start, context_end, queries, keys, values, latent, step_gate, levels, name="attend", cid=0
):
    any_spec = pl.BlockSpec(memory_space=pl.ANY)
    dma = pltpu.SemaphoreType.DMA
    rows = jax.ShapeDtypeStruct(latent.shape, jnp.bfloat16)
    return pl.pallas_call(
        kernel,
        out_shape=(rows, rows, jax.ShapeDtypeStruct((8, step_gate.shape[1]), jnp.float32)),
        in_specs=[any_spec] * 8,
        out_specs=(any_spec, any_spec, pl.BlockSpec(memory_space=pltpu.VMEM)),
        scratch_shapes=[
            pltpu.VMEM((LOCAL_HEADS, BLOCK, HEAD_DIM), jnp.bfloat16),
            pltpu.VMEM((LOCAL_HEADS, 3 * BLOCK, HEAD_DIM), jnp.bfloat16),
            pltpu.VMEM((LOCAL_HEADS, 3 * BLOCK, HEAD_DIM), jnp.bfloat16),
            pltpu.VMEM((LOCAL_HEADS, BLOCK, HEAD_DIM), jnp.bfloat16),
            pltpu.VMEM(step_gate.shape, jnp.float32),
            pltpu.SMEM(context_start.shape, jnp.int32),
            pltpu.SMEM(context_end.shape, jnp.int32),
            pltpu.SMEM(levels.shape, jnp.int32),
            dma((3, LOCAL_HEADS, 8)), dma((3, LOCAL_HEADS)),
            dma((2, LOCAL_HEADS, 2)), dma((2, LOCAL_HEADS, 2)),
            dma((LOCAL_HEADS, 8)), dma((LOCAL_HEADS,)),
            dma((LAT_PARTS,)), dma((LAT_PARTS,)), dma((4,)),
        ],
        compiler_params=pltpu.CompilerParams(
            collective_id=cid, has_side_effects=True, vmem_limit_bytes=61000 << 10
        ),
        cost_estimate=pl.CostEstimate(
            flops=4 * BLOCK * 3 * BLOCK * GROUP, bytes_accessed=8 << 20, transcendentals=0
        ),
        name=name,
    )(context_start, context_end, levels, step_gate, queries, keys, values, latent)


def on_device(queries, keys, values, latent, step_gate, levels, context_start, context_end):
    attended, moved, gate = run_kernel(
        context_start, context_end, queries, keys, values, latent, step_gate, levels
    )
    tiles = (latent.shape[0] // 8, 8, latent.shape[1])
    updated = moved.reshape(tiles).astype(jnp.float32) + gate * attended.reshape(tiles).astype(jnp.float32)
    queued = jnp.where(lax.axis_index("frame") > 0, updated, 0.0).astype(jnp.bfloat16)
    return queued.reshape(latent.shape)


def solution(mesh):
    tokens = P(("frame", "space"), None)
    return jax.shard_map(
        on_device,
        mesh=mesh,
        in_specs=(tokens,) * 4 + (P(),) * 4,
        out_specs=tokens,
        check_vma=False,
    )
```

```python
import functools

import jax
import jax.numpy as jnp
from jax import lax
from jax.experimental import pallas as pl
from jax.experimental.pallas import tpu as pltpu
from jax.sharding import PartitionSpec as P

HEAD_DIM = 128
FRAME_TOK = 64
SLICE = 128
BLOCK = 1024
LOCAL_HEADS = 3
GROUP = LOCAL_HEADS * HEAD_DIM
Q_ROWS = 256
CHUNKS = BLOCK // Q_ROWS
LOG2E = 1.4426950408889634
SCALE2 = HEAD_DIM ** (-0.5) * LOG2E
HIDDEN = -1e30
KEYS, VALUES, QUERIES = 0, 1, 2
MESH = pl.DeviceIdType.MESH
PEERS = 8
LAT_PARTS = 3
NEAR_PARTS = 8


def wrap(a, n):
    return lax.rem(a + n, n)


def position():
    frame, space = lax.axis_index("frame"), lax.axis_index("space")
    return space // 2, frame // 8, lax.rem(frame // 2, 4) + 4 * lax.rem(space, 2), lax.rem(frame, 2)


def device(x, y, z, core):
    return (y * 8 + lax.rem(z, 4) * 2 + core, x * 2 + z // 4)


def following(pair, y, core):
    return (
        wrap(pair + core, 4),
        wrap(y + core * (pair // 3), 8),
        1 - core,
    )


def preceding(pair, y, core):
    back = 1 - core
    return (
        wrap(pair - back, 4),
        wrap(y - back * ((3 - pair) // 3), 8),
        1 - core,
    )


def offset(group):
    return 2 * lax.rem(group, 2)


def worker(pair, y, core, group):
    return device(lax.rem(pair + offset(group), 4), y, group, core)


def kernel(
    start_hbm, end_hbm, levels_hbm, gate_hbm, q_hbm, k_hbm, v_hbm, latent_hbm,
    att_hbm, lat_out_hbm, gate_ref,
    q_buf, k_buf, v_buf, o_buf, gate_buf, start_ref, end_ref, levels_ref,
    in_send, in_recv, near_send, near_recv, o_send, o_recv, lat_send, lat_recv, table_sem,
):
    x, y, z, core = position()
    z_lo, z_hi = lax.rem(z, 4), z // 4
    here = x * 2 + z_hi
    pair = wrap(x - offset(z), 4)
    block = y * 8 + pair * 2 + core
    after, before = following(pair, y, core), preceding(pair, y, core)
    next_worker, prev_worker = worker(*after, z), worker(*before, z)
    home_after, home_before = following(z_lo, y, core), preceding(z_lo, y, core)
    keeps = x == lax.rem(z_lo + offset(z), 4)

    def home(spot, slice_index):
        p, yy, cc = spot
        return device(slice_index // 2, yy, p + 4 * lax.rem(slice_index, 2), cc)

    tables = [
        pltpu.make_async_copy(src, dst, table_sem.at[i])
        for i, (src, dst) in enumerate(
            ((start_hbm, start_ref), (end_hbm, end_ref), (levels_hbm, levels_ref), (gate_hbm, gate_buf))
        )
    ]
    barrier = pltpu.get_barrier_semaphore()

    def greet(target):
        pl.semaphore_signal(barrier, inc=1, device_id=target, device_id_type=MESH)

    for t in range(8):
        source = home((pair, y, core), t)
        pl.when(jnp.logical_not(keeps & (here == t)))(functools.partial(greet, source))
        greet(worker(*home_before, t))
    greet(prev_worker)
    greet(next_worker)
    greet(home(home_before, here))
    pl.semaphore_wait(barrier, jnp.where(keeps, 18, 19))

    arrays = ((k_hbm, k_buf, BLOCK), (v_hbm, v_buf, BLOCK), (q_hbm, q_buf, 0))

    def distance(i):
        turn = lax.rem(i // 2 + x, 4)
        along = 3 - turn if i % 2 else 4 + turn
        return lax.rem(jnp.where(core == 0, along, 8 - along), 8)

    def served(i, act_here, act_there):
        if i % 2:
            mine = keeps & (distance(i) == 0)
            pl.when(mine)(act_here)
            pl.when(jnp.logical_not(mine))(act_there)
        else:
            act_there()

    def incoming(which, h, i):
        hbm, buf, row0 = arrays[which]
        group = lax.rem(z + distance(i), 8)
        return (
            hbm.at[:, pl.ds(pl.multiple_of(group * GROUP + h * HEAD_DIM, HEAD_DIM), HEAD_DIM)],
            buf.at[h, pl.ds(pl.multiple_of(row0 + here * SLICE, SLICE), SLICE)],
            worker(z_lo, y, core, group),
        )

    def in_copy(which, h, i):
        src, dst, target = incoming(which, h, i)
        return pltpu.make_async_remote_copy(
            src_ref=src, dst_ref=dst, send_sem=in_send.at[which, h, i], recv_sem=in_recv.at[which, h],
            device_id=target, device_id_type=MESH,
        )

    def own_copy(which, h, i):
        src, dst, _ = incoming(which, h, i)
        return pltpu.make_async_copy(src, dst, in_recv.at[which, h])

    def send_in(which, h):
        for i in range(PEERS):
            served(i, lambda: own_copy(which, h, i).start(), lambda: in_copy(which, h, i).start())

    def lat_copy(part):
        width = latent_hbm.shape[1] // LAT_PARTS
        columns = pl.ds(pl.multiple_of(part * width, HEAD_DIM), width)
        return pltpu.make_async_remote_copy(
            src_ref=latent_hbm.at[:, columns], dst_ref=lat_out_hbm.at[:, columns],
            send_sem=lat_send.at[part], recv_sem=lat_recv.at[part],
            device_id=home(home_after, here), device_id_type=MESH,
        )

    def wait_in(which, h):
        _, buf, row0 = arrays[which]
        whole = buf.at[h, pl.ds(row0, BLOCK)]
        pltpu.make_async_copy(whole, whole, in_recv.at[which, h]).wait()

    def near_copy(which, h, side, row=0, rows=BLOCK):
        _, buf, _ = arrays[which]
        to = 0 if side else 2 * BLOCK
        return pltpu.make_async_remote_copy(
            src_ref=buf.at[h, pl.ds(BLOCK + row, rows)],
            dst_ref=buf.at[h, pl.ds(to + row, rows)],
            send_sem=near_send.at[which, h, side], recv_sem=near_recv.at[which, h, side],
            device_id=next_worker if side else prev_worker, device_id_type=MESH,
        )

    def pass_on(which, h):
        wait_in(which, h)
        for piece in range(NEAR_PARTS):
            for side in range(2):
                near_copy(which, h, side, piece * (BLOCK // NEAR_PARTS), BLOCK // NEAR_PARTS).start()

    def o_copy(h, t):
        return pltpu.make_async_remote_copy(
            src_ref=o_buf.at[h, pl.ds(pl.multiple_of(t * SLICE, SLICE), SLICE)],
            dst_ref=att_hbm.at[:, pl.ds(pl.multiple_of(z * GROUP + h * HEAD_DIM, HEAD_DIM), HEAD_DIM)],
            send_sem=o_send.at[h, t], recv_sem=o_recv.at[h],
            device_id=home(after, t), device_id_type=MESH,
        )

    for h in range(LOCAL_HEADS):
        for which in (KEYS, VALUES, QUERIES):
            send_in(which, h)
            if which == VALUES:
                lat_copy(h).start()
    for copy in tables:
        copy.start()
    pass_on(KEYS, 0)
    pass_on(VALUES, 0)
    for copy in tables:
        copy.wait()
    level = levels_ref[wrap(lax.axis_index("frame") - 1, 64)]
    gate_ref[...] = jnp.broadcast_to(gate_buf[pl.ds(level, 1), :], gate_ref.shape)

    column = lax.broadcasted_iota(jnp.int32, (1, BLOCK), 1)
    first = start_ref[block] * FRAME_TOK
    last = end_ref[block] * FRAME_TOK
    hide_before = jnp.where((column >= first) & (block > 0), 0.0, HIDDEN)
    hide_after = jnp.where((column < last) & (block < 63), 0.0, HIDDEN)

    def step(n, carry):
        h, i = n // CHUNKS, lax.rem(n, CHUNKS)

        @pl.when(i == 0)
        def _():
            wait_in(QUERIES, h)
            for which in range(2):
                for side in range(2):
                    near_copy(which, h, side).wait_recv()

        @pl.when((i == 2) & (h < LOCAL_HEADS - 1))
        def _():
            pass_on(KEYS, h + 1)

        @pl.when((i == 3) & (h < LOCAL_HEADS - 1))
        def _():
            pass_on(VALUES, h + 1)

        chunk = lax.rem(i + x + z, CHUNKS)
        rows = pl.ds(pl.multiple_of(chunk * Q_ROWS, Q_ROWS), Q_ROWS)
        q = q_buf[h, rows, :]
        parts = []
        for part, hide in ((0, hide_before), (1, None), (2, hide_after)):
            s = lax.dot_general(
                q, k_buf[h, pl.ds(part * BLOCK, BLOCK), :], (((1,), (1,)), ((), ())),
                preferred_element_type=jnp.float32,
            ) * SCALE2
            parts.append(s if hide is None else s + hide)
        top = functools.reduce(jnp.maximum, [jnp.max(s, axis=1, keepdims=True) for s in parts])
        parts = [jnp.exp2(s - top) for s in parts]
        total = sum(jnp.sum(e, axis=1, keepdims=True) for e in parts)
        inverse = 1.0 / total
        out = None
        for part, e in enumerate(parts):
            o = jnp.dot(
                (e * inverse).astype(jnp.bfloat16), v_buf[h, pl.ds(part * BLOCK, BLOCK), :],
                preferred_element_type=jnp.float32,
            )
            out = o if out is None else out + o
        o_buf[h, rows, :] = out.astype(jnp.bfloat16)
        for t in range(Q_ROWS // SLICE):
            o_copy(h, chunk * (Q_ROWS // SLICE) + t).start()
        return carry

    lax.fori_loop(0, LOCAL_HEADS * CHUNKS, step, 0)

    for h in range(LOCAL_HEADS):
        pltpu.make_async_copy(o_buf.at[h], o_buf.at[h], o_recv.at[h]).wait()
    for part in range(LAT_PARTS):
        lat_copy(part).wait()
    for h in range(LOCAL_HEADS):
        for t in range(8):
            o_copy(h, t).wait_send()
        for which in range(3):
            for i in range(PEERS):
                served(i, lambda: None, lambda: in_copy(which, h, i).wait_send())
            if which < 2:
                for side in range(2):
                    near_copy(which, h, side).wait_send()


def run_kernel(
    context_start, context_end, queries, keys, values, latent, step_gate, levels, name="attend", cid=0
):
    any_spec = pl.BlockSpec(memory_space=pl.ANY)
    dma = pltpu.SemaphoreType.DMA
    rows = jax.ShapeDtypeStruct(latent.shape, jnp.bfloat16)
    return pl.pallas_call(
        kernel,
        out_shape=(rows, rows, jax.ShapeDtypeStruct((8, step_gate.shape[1]), jnp.float32)),
        in_specs=[any_spec] * 8,
        out_specs=(any_spec, any_spec, pl.BlockSpec(memory_space=pltpu.VMEM)),
        scratch_shapes=[
            pltpu.VMEM((LOCAL_HEADS, BLOCK, HEAD_DIM), jnp.bfloat16),
            pltpu.VMEM((LOCAL_HEADS, 3 * BLOCK, HEAD_DIM), jnp.bfloat16),
            pltpu.VMEM((LOCAL_HEADS, 3 * BLOCK, HEAD_DIM), jnp.bfloat16),
            pltpu.VMEM((LOCAL_HEADS, BLOCK, HEAD_DIM), jnp.bfloat16),
            pltpu.VMEM(step_gate.shape, jnp.float32),
            pltpu.SMEM(context_start.shape, jnp.int32),
            pltpu.SMEM(context_end.shape, jnp.int32),
            pltpu.SMEM(levels.shape, jnp.int32),
            dma((3, LOCAL_HEADS, 8)), dma((3, LOCAL_HEADS)),
            dma((2, LOCAL_HEADS, 2)), dma((2, LOCAL_HEADS, 2)),
            dma((LOCAL_HEADS, 8)), dma((LOCAL_HEADS,)),
            dma((LAT_PARTS,)), dma((LAT_PARTS,)), dma((4,)),
        ],
        compiler_params=pltpu.CompilerParams(
            collective_id=cid, has_side_effects=True, vmem_limit_bytes=61000 << 10
        ),
        cost_estimate=pl.CostEstimate(
            flops=4 * BLOCK * 3 * BLOCK * GROUP, bytes_accessed=8 << 20, transcendentals=0
        ),
        name=name,
    )(context_start, context_end, levels, step_gate, queries, keys, values, latent)


def on_device(queries, keys, values, latent, step_gate, levels, context_start, context_end):
    attended, moved, gate = run_kernel(
        context_start, context_end, queries, keys, values, latent, step_gate, levels
    )
    tiles = (latent.shape[0] // 8, 8, latent.shape[1])
    updated = moved.reshape(tiles).astype(jnp.float32) + gate * attended.reshape(tiles).astype(jnp.float32)
    queued = jnp.where(lax.axis_index("frame") > 0, updated, 0.0).astype(jnp.bfloat16)
    return queued.reshape(latent.shape)


def solution(mesh):
    tokens = P(("frame", "space"), None)
    return jax.shard_map(
        on_device,
        mesh=mesh,
        in_specs=(tokens,) * 4 + (P(),) * 4,
        out_specs=tokens,
        check_vma=False,
    )
```

```python
import functools

import jax
import jax.numpy as jnp
from jax import lax
from jax.experimental import pallas as pl
from jax.experimental.pallas import tpu as pltpu
from jax.sharding import PartitionSpec as P

HEAD_DIM = 128
FRAME_TOK = 64
SLICE = 128
BLOCK = 1024
LOCAL_HEADS = 3
GROUP = LOCAL_HEADS * HEAD_DIM
Q_ROWS = 256
CHUNKS = BLOCK // Q_ROWS
LOG2E = 1.4426950408889634
SCALE2 = HEAD_DIM ** (-0.5) * LOG2E
HIDDEN = -1e30
KEYS, VALUES, QUERIES = 0, 1, 2
MESH = pl.DeviceIdType.MESH
PEERS = 8
LAT_PARTS = 3
NEAR_PARTS = 8


def wrap(a, n):
    return lax.rem(a + n, n)


def position():
    frame, space = lax.axis_index("frame"), lax.axis_index("space")
    return space // 2, frame // 8, lax.rem(frame // 2, 4) + 4 * lax.rem(space, 2), lax.rem(frame, 2)


def device(x, y, z, core):
    return (y * 8 + lax.rem(z, 4) * 2 + core, x * 2 + z // 4)


def following(pair, y, core):
    return (
        wrap(pair + core, 4),
        wrap(y + core * (pair // 3), 8),
        1 - core,
    )


def preceding(pair, y, core):
    back = 1 - core
    return (
        wrap(pair - back, 4),
        wrap(y - back * ((3 - pair) // 3), 8),
        1 - core,
    )


def offset(group):
    return 2 * lax.rem(group, 2)


def worker(pair, y, core, group):
    return device(lax.rem(pair + offset(group), 4), y, group, core)


def kernel(
    start_hbm, end_hbm, levels_hbm, gate_hbm, q_hbm, k_hbm, v_hbm, latent_hbm,
    out_hbm,
    att_buf, lat_buf, out_buf, gate_row,
    q_buf, k_buf, v_buf, o_buf, gate_buf, start_ref, end_ref, levels_ref,
    in_send, in_recv, near_send, near_recv, o_send, o_recv, lat_send, lat_recv, table_sem, out_sem,
):
    x, y, z, core = position()
    z_lo, z_hi = lax.rem(z, 4), z // 4
    here = x * 2 + z_hi
    pair = wrap(x - offset(z), 4)
    block = y * 8 + pair * 2 + core
    after, before = following(pair, y, core), preceding(pair, y, core)
    next_worker, prev_worker = worker(*after, z), worker(*before, z)
    home_after, home_before = following(z_lo, y, core), preceding(z_lo, y, core)
    keeps = x == lax.rem(z_lo + offset(z), 4)

    def home(spot, slice_index):
        p, yy, cc = spot
        return device(slice_index // 2, yy, p + 4 * lax.rem(slice_index, 2), cc)

    tables = [
        pltpu.make_async_copy(src, dst, table_sem.at[i])
        for i, (src, dst) in enumerate(
            ((start_hbm, start_ref), (end_hbm, end_ref), (levels_hbm, levels_ref), (gate_hbm, gate_buf))
        )
    ]
    barrier = pltpu.get_barrier_semaphore()

    def greet(target):
        pl.semaphore_signal(barrier, inc=1, device_id=target, device_id_type=MESH)

    for t in range(8):
        source = home((pair, y, core), t)
        pl.when(jnp.logical_not(keeps & (here == t)))(functools.partial(greet, source))
        greet(worker(*home_before, t))
    greet(prev_worker)
    greet(next_worker)
    greet(home(home_before, here))
    pl.semaphore_wait(barrier, jnp.where(keeps, 18, 19))

    arrays = ((k_hbm, k_buf, BLOCK), (v_hbm, v_buf, BLOCK), (q_hbm, q_buf, 0))

    def distance(i):
        turn = lax.rem(i // 2 + x, 4)
        along = 3 - turn if i % 2 else 4 + turn
        return lax.rem(jnp.where(core == 0, along, 8 - along), 8)

    def served(i, act_here, act_there):
        if i % 2:
            mine = keeps & (distance(i) == 0)
            pl.when(mine)(act_here)
            pl.when(jnp.logical_not(mine))(act_there)
        else:
            act_there()

    def incoming(which, h, i):
        hbm, buf, row0 = arrays[which]
        group = lax.rem(z + distance(i), 8)
        return (
            hbm.at[:, pl.ds(pl.multiple_of(group * GROUP + h * HEAD_DIM, HEAD_DIM), HEAD_DIM)],
            buf.at[h, pl.ds(pl.multiple_of(row0 + here * SLICE, SLICE), SLICE)],
            worker(z_lo, y, core, group),
        )

    def in_copy(which, h, i):
        src, dst, target = incoming(which, h, i)
        return pltpu.make_async_remote_copy(
            src_ref=src, dst_ref=dst, send_sem=in_send.at[which, h, i], recv_sem=in_recv.at[which, h],
            device_id=target, device_id_type=MESH,
        )

    def own_copy(which, h, i):
        src, dst, _ = incoming(which, h, i)
        return pltpu.make_async_copy(src, dst, in_recv.at[which, h])

    def send_in(which, h):
        for i in range(PEERS):
            served(i, lambda: own_copy(which, h, i).start(), lambda: in_copy(which, h, i).start())

    def lat_copy(part):
        width = latent_hbm.shape[1] // LAT_PARTS
        columns = pl.ds(pl.multiple_of(part * width, HEAD_DIM), width)
        return pltpu.make_async_remote_copy(
            src_ref=latent_hbm.at[:, columns], dst_ref=lat_buf.at[:, columns],
            send_sem=lat_send.at[part], recv_sem=lat_recv.at[part],
            device_id=home(home_after, here), device_id_type=MESH,
        )

    def wait_in(which, h):
        _, buf, row0 = arrays[which]
        whole = buf.at[h, pl.ds(row0, BLOCK)]
        pltpu.make_async_copy(whole, whole, in_recv.at[which, h]).wait()

    def near_copy(which, h, side, row=0, rows=BLOCK):
        _, buf, _ = arrays[which]
        to = 0 if side else 2 * BLOCK
        return pltpu.make_async_remote_copy(
            src_ref=buf.at[h, pl.ds(BLOCK + row, rows)],
            dst_ref=buf.at[h, pl.ds(to + row, rows)],
            send_sem=near_send.at[which, h, side], recv_sem=near_recv.at[which, h, side],
            device_id=next_worker if side else prev_worker, device_id_type=MESH,
        )

    def pass_on(which, h):
        wait_in(which, h)
        for piece in range(NEAR_PARTS):
            for side in range(2):
                near_copy(which, h, side, piece * (BLOCK // NEAR_PARTS), BLOCK // NEAR_PARTS).start()

    def o_copy(h, t):
        return pltpu.make_async_remote_copy(
            src_ref=o_buf.at[h, pl.ds(pl.multiple_of(t * SLICE, SLICE), SLICE)],
            dst_ref=att_buf.at[:, pl.ds(pl.multiple_of(z * GROUP + h * HEAD_DIM, HEAD_DIM), HEAD_DIM)],
            send_sem=o_send.at[h, t], recv_sem=o_recv.at[h],
            device_id=home(after, t), device_id_type=MESH,
        )

    for h in range(LOCAL_HEADS):
        for which in (KEYS, VALUES, QUERIES):
            send_in(which, h)
            if which == VALUES:
                lat_copy(h).start()
    for copy in tables:
        copy.start()
    pass_on(KEYS, 0)
    pass_on(VALUES, 0)
    for copy in tables:
        copy.wait()
    level = levels_ref[wrap(lax.axis_index("frame") - 1, 64)]
    gate_row[...] = jnp.broadcast_to(gate_buf[pl.ds(level, 1), :], gate_row.shape)

    column = lax.broadcasted_iota(jnp.int32, (1, BLOCK), 1)
    first = start_ref[block] * FRAME_TOK
    last = end_ref[block] * FRAME_TOK
    hide_before = jnp.where((column >= first) & (block > 0), 0.0, HIDDEN)
    hide_after = jnp.where((column < last) & (block < 63), 0.0, HIDDEN)

    def step(n, carry):
        h, i = n // CHUNKS, lax.rem(n, CHUNKS)

        @pl.when(i == 0)
        def _():
            wait_in(QUERIES, h)
            for which in range(2):
                for side in range(2):
                    near_copy(which, h, side).wait_recv()

        @pl.when((i == 2) & (h < LOCAL_HEADS - 1))
        def _():
            pass_on(KEYS, h + 1)

        @pl.when((i == 3) & (h < LOCAL_HEADS - 1))
        def _():
            pass_on(VALUES, h + 1)

        chunk = lax.rem(i + x + z, CHUNKS)
        rows = pl.ds(pl.multiple_of(chunk * Q_ROWS, Q_ROWS), Q_ROWS)
        q = q_buf[h, rows, :]
        parts = []
        for part, hide in ((0, hide_before), (1, None), (2, hide_after)):
            s = lax.dot_general(
                q, k_buf[h, pl.ds(part * BLOCK, BLOCK), :], (((1,), (1,)), ((), ())),
                preferred_element_type=jnp.float32,
            ) * SCALE2
            parts.append(s if hide is None else s + hide)
        top = functools.reduce(jnp.maximum, [jnp.max(s, axis=1, keepdims=True) for s in parts])
        parts = [jnp.exp2(s - top) for s in parts]
        total = sum(jnp.sum(e, axis=1, keepdims=True) for e in parts)
        inverse = 1.0 / total
        out = None
        for part, e in enumerate(parts):
            o = jnp.dot(
                (e * inverse).astype(jnp.bfloat16), v_buf[h, pl.ds(part * BLOCK, BLOCK), :],
                preferred_element_type=jnp.float32,
            )
            out = o if out is None else out + o
        o_buf[h, rows, :] = out.astype(jnp.bfloat16)
        for t in range(Q_ROWS // SLICE):
            o_copy(h, chunk * (Q_ROWS // SLICE) + t).start()
        return carry

    lax.fori_loop(0, LOCAL_HEADS * CHUNKS, step, 0)

    for h in range(LOCAL_HEADS):
        for which in range(3):
            for i in range(PEERS):
                served(i, lambda: None, lambda: in_copy(which, h, i).wait_send())
            if which < 2:
                for side in range(2):
                    near_copy(which, h, side).wait_send()
    for part in range(LAT_PARTS):
        lat_copy(part).wait()
    moved = lax.axis_index("frame") > 0
    for h in range(LOCAL_HEADS):
        for t in range(PEERS):
            o_copy(h, t).wait_send()
        pltpu.make_async_copy(o_buf.at[h], o_buf.at[h], o_recv.at[h]).wait()
        for group in range(PEERS):
            columns = pl.ds(group * GROUP + h * HEAD_DIM, HEAD_DIM)
            updated = lat_buf[:, columns].astype(jnp.float32) + gate_row[0:1, columns] * att_buf[
                :, columns
            ].astype(jnp.float32)
            out_buf[:, columns] = jnp.where(moved, updated, 0.0).astype(jnp.bfloat16)
    done = pltpu.make_async_copy(out_buf, out_hbm, out_sem)
    done.start()
    done.wait()


def run_kernel(
    context_start, context_end, queries, keys, values, latent, step_gate, levels, name="attend", cid=0
):
    any_spec = pl.BlockSpec(memory_space=pl.ANY)
    dma = pltpu.SemaphoreType.DMA
    rows = jax.ShapeDtypeStruct(latent.shape, jnp.bfloat16)
    return pl.pallas_call(
        kernel,
        out_shape=rows,
        in_specs=[any_spec] * 8,
        out_specs=any_spec,
        scratch_shapes=[
            pltpu.VMEM(rows.shape, jnp.bfloat16),
            pltpu.VMEM(rows.shape, jnp.bfloat16),
            pltpu.VMEM(rows.shape, jnp.bfloat16),
            pltpu.VMEM((8, step_gate.shape[1]), jnp.float32),
            pltpu.VMEM((LOCAL_HEADS, BLOCK, HEAD_DIM), jnp.bfloat16),
            pltpu.VMEM((LOCAL_HEADS, 3 * BLOCK, HEAD_DIM), jnp.bfloat16),
            pltpu.VMEM((LOCAL_HEADS, 3 * BLOCK, HEAD_DIM), jnp.bfloat16),
            pltpu.VMEM((LOCAL_HEADS, BLOCK, HEAD_DIM), jnp.bfloat16),
            pltpu.VMEM(step_gate.shape, jnp.float32),
            pltpu.SMEM(context_start.shape, jnp.int32),
            pltpu.SMEM(context_end.shape, jnp.int32),
            pltpu.SMEM(levels.shape, jnp.int32),
            dma((3, LOCAL_HEADS, 8)), dma((3, LOCAL_HEADS)),
            dma((2, LOCAL_HEADS, 2)), dma((2, LOCAL_HEADS, 2)),
            dma((LOCAL_HEADS, 8)), dma((LOCAL_HEADS,)),
            dma((LAT_PARTS,)), dma((LAT_PARTS,)), dma((4,)), dma,
        ],
        compiler_params=pltpu.CompilerParams(
            collective_id=cid, has_side_effects=True, vmem_limit_bytes=61000 << 10
        ),
        cost_estimate=pl.CostEstimate(
            flops=4 * BLOCK * 3 * BLOCK * GROUP, bytes_accessed=8 << 20, transcendentals=0
        ),
        name=name,
    )(context_start, context_end, levels, step_gate, queries, keys, values, latent)


def on_device(queries, keys, values, latent, step_gate, levels, context_start, context_end):
    return run_kernel(context_start, context_end, queries, keys, values, latent, step_gate, levels)


def solution(mesh):
    tokens = P(("frame", "space"), None)
    return jax.shard_map(
        on_device,
        mesh=mesh,
        in_specs=(tokens,) * 4 + (P(),) * 4,
        out_specs=tokens,
        check_vma=False,
    )
```

```python
import functools

import jax
import jax.numpy as jnp
from jax import lax
from jax.experimental import pallas as pl
from jax.experimental.pallas import tpu as pltpu
from jax.sharding import PartitionSpec as P

HEAD_DIM = 128
FRAME_TOK = 64
SLICE = 128
BLOCK = 1024
LOCAL_HEADS = 3
GROUP = LOCAL_HEADS * HEAD_DIM
Q_ROWS = 256
CHUNKS = BLOCK // Q_ROWS
LOG2E = 1.4426950408889634
SCALE2 = HEAD_DIM ** (-0.5) * LOG2E
HIDDEN = -1e30
KEYS, VALUES, QUERIES = 0, 1, 2
MESH = pl.DeviceIdType.MESH
PEERS = 8
LAT_PARTS = 3
NEAR_PARTS = 8


def wrap(a, n):
    return lax.rem(a + n, n)


def position():
    frame, space = lax.axis_index("frame"), lax.axis_index("space")
    return space // 2, frame // 8, lax.rem(frame // 2, 4) + 4 * lax.rem(space, 2), lax.rem(frame, 2)


def device(x, y, z, core):
    return (y * 8 + lax.rem(z, 4) * 2 + core, x * 2 + z // 4)


def following(pair, y, core):
    return (
        wrap(pair + core, 4),
        wrap(y + core * (pair // 3), 8),
        1 - core,
    )


def preceding(pair, y, core):
    back = 1 - core
    return (
        wrap(pair - back, 4),
        wrap(y - back * ((3 - pair) // 3), 8),
        1 - core,
    )


def offset(group):
    return 2 * lax.rem(group, 2) + group // 4


def worker(pair, y, core, group):
    return device(lax.rem(pair + offset(group), 4), y, group, core)


def kernel(
    start_hbm, end_hbm, levels_hbm, gate_hbm, q_hbm, k_hbm, v_hbm, latent_hbm,
    out_hbm,
    att_buf, lat_buf, out_buf, gate_row,
    q_buf, k_buf, v_buf, o_buf, gate_buf, start_ref, end_ref, levels_ref,
    in_send, in_recv, near_send, near_recv, o_send, o_recv, lat_send, lat_recv, table_sem, out_sem,
):
    x, y, z, core = position()
    z_lo, z_hi = lax.rem(z, 4), z // 4
    here = x * 2 + z_hi
    pair = wrap(x - offset(z), 4)
    block = y * 8 + pair * 2 + core
    after, before = following(pair, y, core), preceding(pair, y, core)
    next_worker, prev_worker = worker(*after, z), worker(*before, z)
    home_after, home_before = following(z_lo, y, core), preceding(z_lo, y, core)
    keeps = x == lax.rem(z_lo + offset(z), 4)

    def home(spot, slice_index):
        p, yy, cc = spot
        return device(slice_index // 2, yy, p + 4 * lax.rem(slice_index, 2), cc)

    tables = [
        pltpu.make_async_copy(src, dst, table_sem.at[i])
        for i, (src, dst) in enumerate(
            ((start_hbm, start_ref), (end_hbm, end_ref), (levels_hbm, levels_ref), (gate_hbm, gate_buf))
        )
    ]
    barrier = pltpu.get_barrier_semaphore()

    def greet(target):
        pl.semaphore_signal(barrier, inc=1, device_id=target, device_id_type=MESH)

    for t in range(8):
        source = home((pair, y, core), t)
        pl.when(jnp.logical_not(keeps & (here == t)))(functools.partial(greet, source))
        greet(worker(*home_before, t))
    greet(prev_worker)
    greet(next_worker)
    greet(home(home_before, here))
    pl.semaphore_wait(barrier, jnp.where(keeps, 18, 19))

    arrays = ((k_hbm, k_buf, BLOCK), (v_hbm, v_buf, BLOCK), (q_hbm, q_buf, 0))

    def distance(i):
        turn = lax.rem(i // 2 + x, 4)
        along = 3 - turn if i % 2 else 4 + turn
        return lax.rem(jnp.where(core == 0, along, 8 - along), 8)

    def served(i, act_here, act_there):
        if i % 2:
            mine = keeps & (distance(i) == 0)
            pl.when(mine)(act_here)
            pl.when(jnp.logical_not(mine))(act_there)
        else:
            act_there()

    def incoming(which, h, i):
        hbm, buf, row0 = arrays[which]
        group = lax.rem(z + distance(i), 8)
        return (
            hbm.at[:, pl.ds(pl.multiple_of(group * GROUP + h * HEAD_DIM, HEAD_DIM), HEAD_DIM)],
            buf.at[h, pl.ds(pl.multiple_of(row0 + here * SLICE, SLICE), SLICE)],
            worker(z_lo, y, core, group),
        )

    def in_copy(which, h, i):
        src, dst, target = incoming(which, h, i)
        return pltpu.make_async_remote_copy(
            src_ref=src, dst_ref=dst, send_sem=in_send.at[which, h, i], recv_sem=in_recv.at[which, h],
            device_id=target, device_id_type=MESH,
        )

    def own_copy(which, h, i):
        src, dst, _ = incoming(which, h, i)
        return pltpu.make_async_copy(src, dst, in_recv.at[which, h])

    def send_in(which, h):
        for i in range(PEERS):
            served(i, lambda: own_copy(which, h, i).start(), lambda: in_copy(which, h, i).start())

    def lat_copy(part):
        width = latent_hbm.shape[1] // LAT_PARTS
        columns = pl.ds(pl.multiple_of(part * width, HEAD_DIM), width)
        return pltpu.make_async_remote_copy(
            src_ref=latent_hbm.at[:, columns], dst_ref=lat_buf.at[:, columns],
            send_sem=lat_send.at[part], recv_sem=lat_recv.at[part],
            device_id=home(home_after, here), device_id_type=MESH,
        )

    def wait_in(which, h):
        _, buf, row0 = arrays[which]
        whole = buf.at[h, pl.ds(row0, BLOCK)]
        pltpu.make_async_copy(whole, whole, in_recv.at[which, h]).wait()

    def near_copy(which, h, side, row=0, rows=BLOCK):
        _, buf, _ = arrays[which]
        to = 0 if side else 2 * BLOCK
        return pltpu.make_async_remote_copy(
            src_ref=buf.at[h, pl.ds(BLOCK + row, rows)],
            dst_ref=buf.at[h, pl.ds(to + row, rows)],
            send_sem=near_send.at[which, h, side], recv_sem=near_recv.at[which, h, side],
            device_id=next_worker if side else prev_worker, device_id_type=MESH,
        )

    def pass_on(which, h):
        wait_in(which, h)
        for piece in range(NEAR_PARTS):
            for side in range(2):
                near_copy(which, h, side, piece * (BLOCK // NEAR_PARTS), BLOCK // NEAR_PARTS).start()

    def o_copy(h, t):
        return pltpu.make_async_remote_copy(
            src_ref=o_buf.at[h, pl.ds(pl.multiple_of(t * SLICE, SLICE), SLICE)],
            dst_ref=att_buf.at[:, pl.ds(pl.multiple_of(z * GROUP + h * HEAD_DIM, HEAD_DIM), HEAD_DIM)],
            send_sem=o_send.at[h, t], recv_sem=o_recv.at[h],
            device_id=home(after, t), device_id_type=MESH,
        )

    for h in range(LOCAL_HEADS):
        for which in (KEYS, VALUES, QUERIES):
            send_in(which, h)
    for copy in tables:
        copy.start()
    pass_on(KEYS, 0)
    pass_on(VALUES, 0)
    lat_copy(0).start()
    for copy in tables:
        copy.wait()
    level = levels_ref[wrap(lax.axis_index("frame") - 1, 64)]
    gate_row[...] = jnp.broadcast_to(gate_buf[pl.ds(level, 1), :], gate_row.shape)

    column = lax.broadcasted_iota(jnp.int32, (1, BLOCK), 1)
    first = start_ref[block] * FRAME_TOK
    last = end_ref[block] * FRAME_TOK
    hide_before = jnp.where((column >= first) & (block > 0), 0.0, HIDDEN)
    hide_after = jnp.where((column < last) & (block < 63), 0.0, HIDDEN)

    def step(n, carry):
        h, i = n // CHUNKS, lax.rem(n, CHUNKS)

        @pl.when(i == 0)
        def _():
            wait_in(QUERIES, h)
            for which in range(2):
                for side in range(2):
                    near_copy(which, h, side).wait_recv()

        @pl.when((i == 2) & (h < LOCAL_HEADS - 1))
        def _():
            pass_on(KEYS, h + 1)

        @pl.when((i == 3) & (h < LOCAL_HEADS - 1))
        def _():
            pass_on(VALUES, h + 1)
            lat_copy(h + 1).start()

        chunk = lax.rem(i + x + z, CHUNKS)
        rows = pl.ds(pl.multiple_of(chunk * Q_ROWS, Q_ROWS), Q_ROWS)
        q = q_buf[h, rows, :]
        parts = []
        for part, hide in ((0, hide_before), (1, None), (2, hide_after)):
            s = lax.dot_general(
                q, k_buf[h, pl.ds(part * BLOCK, BLOCK), :], (((1,), (1,)), ((), ())),
                preferred_element_type=jnp.float32,
            ) * SCALE2
            parts.append(s if hide is None else s + hide)
        top = functools.reduce(jnp.maximum, [jnp.max(s, axis=1, keepdims=True) for s in parts])
        parts = [jnp.exp2(s - top) for s in parts]
        total = sum(jnp.sum(e, axis=1, keepdims=True) for e in parts)
        inverse = 1.0 / total
        out = None
        for part, e in enumerate(parts):
            o = jnp.dot(
                (e * inverse).astype(jnp.bfloat16), v_buf[h, pl.ds(part * BLOCK, BLOCK), :],
                preferred_element_type=jnp.float32,
            )
            out = o if out is None else out + o
        o_buf[h, rows, :] = out.astype(jnp.bfloat16)
        for t in range(Q_ROWS // SLICE):
            o_copy(h, chunk * (Q_ROWS // SLICE) + t).start()
        return carry

    lax.fori_loop(0, LOCAL_HEADS * CHUNKS, step, 0)

    for h in range(LOCAL_HEADS):
        for which in range(3):
            for i in range(PEERS):
                served(i, lambda: None, lambda: in_copy(which, h, i).wait_send())
            if which < 2:
                for side in range(2):
                    near_copy(which, h, side).wait_send()
    for part in range(LAT_PARTS):
        lat_copy(part).wait()
    moved = lax.axis_index("frame") > 0
    for h in range(LOCAL_HEADS):
        for t in range(PEERS):
            o_copy(h, t).wait_send()
        pltpu.make_async_copy(o_buf.at[h], o_buf.at[h], o_recv.at[h]).wait()
        for group in range(PEERS):
            columns = pl.ds(group * GROUP + h * HEAD_DIM, HEAD_DIM)
            updated = lat_buf[:, columns].astype(jnp.float32) + gate_row[0:1, columns] * att_buf[
                :, columns
            ].astype(jnp.float32)
            out_buf[:, columns] = jnp.where(moved, updated, 0.0).astype(jnp.bfloat16)
    done = pltpu.make_async_copy(out_buf, out_hbm, out_sem)
    done.start()
    done.wait()


def run_kernel(
    context_start, context_end, queries, keys, values, latent, step_gate, levels, name="attend", cid=0
):
    any_spec = pl.BlockSpec(memory_space=pl.ANY)
    dma = pltpu.SemaphoreType.DMA
    rows = jax.ShapeDtypeStruct(latent.shape, jnp.bfloat16)
    return pl.pallas_call(
        kernel,
        out_shape=rows,
        in_specs=[any_spec] * 8,
        out_specs=any_spec,
        scratch_shapes=[
            pltpu.VMEM(rows.shape, jnp.bfloat16),
            pltpu.VMEM(rows.shape, jnp.bfloat16),
            pltpu.VMEM(rows.shape, jnp.bfloat16),
            pltpu.VMEM((8, step_gate.shape[1]), jnp.float32),
            pltpu.VMEM((LOCAL_HEADS, BLOCK, HEAD_DIM), jnp.bfloat16),
            pltpu.VMEM((LOCAL_HEADS, 3 * BLOCK, HEAD_DIM), jnp.bfloat16),
            pltpu.VMEM((LOCAL_HEADS, 3 * BLOCK, HEAD_DIM), jnp.bfloat16),
            pltpu.VMEM((LOCAL_HEADS, BLOCK, HEAD_DIM), jnp.bfloat16),
            pltpu.VMEM(step_gate.shape, jnp.float32),
            pltpu.SMEM(context_start.shape, jnp.int32),
            pltpu.SMEM(context_end.shape, jnp.int32),
            pltpu.SMEM(levels.shape, jnp.int32),
            dma((3, LOCAL_HEADS, 8)), dma((3, LOCAL_HEADS)),
            dma((2, LOCAL_HEADS, 2)), dma((2, LOCAL_HEADS, 2)),
            dma((LOCAL_HEADS, 8)), dma((LOCAL_HEADS,)),
            dma((LAT_PARTS,)), dma((LAT_PARTS,)), dma((4,)), dma,
        ],
        compiler_params=pltpu.CompilerParams(
            collective_id=cid, has_side_effects=True, vmem_limit_bytes=61000 << 10
        ),
        cost_estimate=pl.CostEstimate(
            flops=4 * BLOCK * 3 * BLOCK * GROUP, bytes_accessed=8 << 20, transcendentals=0
        ),
        name=name,
    )(context_start, context_end, levels, step_gate, queries, keys, values, latent)


def on_device(queries, keys, values, latent, step_gate, levels, context_start, context_end):
    return run_kernel(context_start, context_end, queries, keys, values, latent, step_gate, levels)


def solution(mesh):
    tokens = P(("frame", "space"), None)
    return jax.shard_map(
        on_device,
        mesh=mesh,
        in_specs=(tokens,) * 4 + (P(),) * 4,
        out_specs=tokens,
        check_vma=False,
    )
```
